256 devices in a mesh: pair: 2 (over core), rep: 32 (over z, x), slab: 4 (over y).
Axes of the slice: x: 4, y: 4, z: 8, core: 2. Of those that a mesh axis runs over, the one named last changes fastest.
Arguments:
- amplitudes: bfloat16 [16384, 4096], P(('pair', 'slab'), 'rep'), may hold values from -6 to 6
- tile_pairs: int32 [16384], P(('pair', 'slab')), may hold values from 0 to 15, as said below
- row_pairs: int32 [16384], P(('pair', 'slab')), may hold values from 0 to 255
- owner: int32 [16], replicated, may hold values from 0 to 15, as said below
- integrals: bfloat16 [2, 16, 4096, 4096], P(None, 'pair', 'rep', 'slab'), may hold values from -0.0625 to 0.0625
Outputs:
- ladder: bfloat16 [2048, 2, 4096], P(('pair', 'slab'), None, 'rep')
The draws below stay inside these ranges and needn't reach their ends.
Inputs may be any that keep to these rules, and one draw needn't show every extreme that they name: Each occupied pair of a device is named by exactly 8 of its rows, with distinct tile pairs. Call slots p * 8 to (p + 1) * 8 - 1 owner block p. At most 6 tiles of one occupied pair have slots owner[tile_pairs] in one owner block; in the rows of one device at most 1536 do, and every device reaches 1536 for some block. `owner`: each value once.
All inputs are finite; a program needn't handle non-finite values.
Results may differ from the reference program's by a relative error of at most 0.001.
Values may be sent and summed in bfloat16 or wider, within the bound.
No kernel may reach another device: no remote copies, remote signals or barrier semaphores. Data moves between devices by JAX's collectives and lax.ppermute only.
A program may use at most 128 MiB of HBM per device.

```python
import jax
import jax.numpy as jnp
from jax import lax

TW = 4096
DOMAIN = 8
HOME = 6
NP = 16
NC = 2
PAIRS_DEV = 256
ROWS_DEV = 2048
BLOCKS = 8
ROWS = 16384
N_PAIR = 2
N_SLAB = 4


def common_draw(key):
    key = jax.random.fold_in(key, 11)
    keys = jax.random.split(key, 8)
    owner = jax.random.permutation(keys[0], NP).astype(jnp.int32)
    block_ids = jnp.arange(BLOCKS, dtype=jnp.int32)
    slab_ids = block_ids % N_SLAB
    offset = jax.random.randint(keys[1], (), 0, N_PAIR)
    forced = jax.random.randint(keys[2], (), 0, N_SLAB)
    shared = (jax.random.randint(keys[3], (N_SLAB,), 0, 2) == 1) | (jnp.arange(N_SLAB) == forced)
    loose = jax.random.randint(keys[4], (BLOCKS,), 0, N_PAIR)
    homes = jnp.where(shared[slab_ids], (slab_ids + offset) % N_PAIR, loose)
    width = NP // N_PAIR
    near_scores = jax.random.randint(keys[5], (BLOCKS, PAIRS_DEV, width), 0, 1 << 16) * width + jnp.arange(width, dtype=jnp.int32)
    near = jnp.argsort(near_scores, axis=-1)[..., :HOME]
    far_count = NP - width
    far_scores = jax.random.randint(keys[6], (BLOCKS, PAIRS_DEV, far_count), 0, 1 << 16) * far_count + jnp.arange(far_count, dtype=jnp.int32)
    far = jnp.argsort(far_scores, axis=-1)[..., :DOMAIN - HOME]
    base = (homes * width)[:, None, None]
    slot_table = jnp.concatenate([base + near, (base + width + far) % NP], axis=-1).astype(jnp.int32)
    pair_table = jnp.broadcast_to(jnp.arange(PAIRS_DEV, dtype=jnp.int32)[None, :, None], slot_table.shape)
    slot_rows = slot_table.reshape(BLOCKS, ROWS_DEV)
    pair_rows = pair_table.reshape(BLOCKS, ROWS_DEV)
    order_scores = jax.random.randint(keys[7], (BLOCKS, ROWS_DEV), 0, 1 << 16) * ROWS_DEV + jnp.arange(ROWS_DEV, dtype=jnp.int32)
    order = jnp.argsort(order_scores, axis=-1)
    slot_rows = jnp.take_along_axis(slot_rows, order, axis=-1)
    pair_rows = jnp.take_along_axis(pair_rows, order, axis=-1)
    inverse = jnp.argsort(owner).astype(jnp.int32)
    tile_pairs = inverse[slot_rows].reshape(-1).astype(jnp.int32)
    row_pairs = pair_rows.reshape(-1).astype(jnp.int32)
    return (owner, tile_pairs, row_pairs)


def draw_owner(key, part):
    return common_draw(key)[0]


def draw_tile_pairs(key, part):
    return common_draw(key)[1]


def draw_row_pairs(key, part):
    return common_draw(key)[2]


def spiked(drawn, own_key, source, target, shards_of, factor):
    def block_of(dim):
        return (jnp.arange(drawn.shape[dim]) // (drawn.shape[dim] // shards_of)).reshape((-1,) + (1,) * (drawn.ndim - 1 - dim))

    first = jax.random.permutation(own_key, shards_of)[block_of(target)]
    second = (block_of(target) + shards_of // 2) % shards_of
    return jnp.where((block_of(source) == first) | (block_of(source) == second), factor * drawn, drawn)


def levels(rng, dims, cuts, smallest, top_value):
    loudness, own = 1.0, jax.random.fold_in(rng, 6)
    for dim, shards_of in cuts:
        steps = jnp.exp(jax.random.uniform(jax.random.fold_in(own, dim), (shards_of,), jnp.float32, smallest / len(cuts), top_value / len(cuts)))
        loudness = loudness * jnp.repeat(steps, dims[dim] // shards_of).reshape([-1 if axis == dim else 1 for axis in range(len(dims))])
    return loudness


def centred(rng, dims, spread, most, shards=(), kind=jnp.bfloat16):
    entries = jax.random.normal(rng, dims, jnp.float32) * spread
    if len(shards) > 0:
        entries = levels(rng, dims, shards, -0.22, 0.18) * entries
    return jnp.clip(entries, min=-most, max=most).astype(kind)


def heavy_noise(stream_key, dims, deviation, bound, shards, heavy, kind=jnp.bfloat16):
    array = deviation * jax.random.normal(stream_key, dims, jnp.float32)
    if shards:
        array = array * levels(stream_key, dims, shards, -0.22, 0.18)
    return jnp.clip(spiked(array, jax.random.fold_in(stream_key, 3), *heavy), -bound, bound).astype(kind)


def setup_inputs(seed: int = 0) -> dict:
    key_list = jax.random.split(jax.random.key(seed), 6)
    amplitudes = centred(key_list[0], (ROWS, TW), 1.0, 6.0, ((0, 8), (1, 32)))
    tile_pairs = draw_tile_pairs(jax.random.fold_in(key_list[5], 71), 0)
    row_pairs = draw_row_pairs(jax.random.fold_in(key_list[5], 71), 0)
    owner = draw_owner(jax.random.fold_in(key_list[5], 71), 0)
    integrals = heavy_noise(key_list[4], (NC, NP, TW, TW), (TW * DOMAIN) ** -0.5, 0.0625, ((1, 2), (2, 32), (3, 4)), (2, 3, 32, 2.75))
    return {"amplitudes": amplitudes, "tile_pairs": tile_pairs, "row_pairs": row_pairs, "owner": owner, "integrals": integrals}


def reference(amplitudes, tile_pairs, row_pairs, owner, integrals):
    row_count = amplitudes.shape[0]
    tile_count = owner.shape[0]
    out_count = integrals.shape[0]
    blocks = jnp.arange(row_count, dtype=jnp.int32) // ROWS_DEV
    pair_id = (blocks * PAIRS_DEV + row_pairs).astype(jnp.int32)
    slots = owner[tile_pairs].astype(jnp.int32)
    total_pairs = PAIRS_DEV * N_PAIR * N_SLAB
    table = jnp.full((total_pairs * tile_count,), row_count, jnp.int32)
    table = table.at[pair_id * tile_count + slots].set(jnp.arange(row_count, dtype=jnp.int32))
    table = table.reshape(total_pairs, tile_count)
    padded = jnp.concatenate([amplitudes, jnp.zeros((1, amplitudes.shape[1]), amplitudes.dtype)], axis=0)

    def add_slot(total, slot_index):
        picked = lax.dynamic_index_in_dim(table, slot_index, 1, keepdims=False).astype(jnp.int32)
        rows = jnp.take(padded, picked, axis=0)
        block = lax.dynamic_index_in_dim(integrals, slot_index, 1, keepdims=False)
        terms = jnp.stack([jnp.dot(rows, block[c], preferred_element_type=jnp.float32) for c in range(out_count)], axis=1)
        return total + terms, None

    start = jnp.zeros((total_pairs, out_count, amplitudes.shape[1]), jnp.float32)
    total, _ = lax.scan(add_slot, start, jnp.arange(tile_count, dtype=jnp.int32))
    return total.astype(jnp.bfloat16)
```

```python
import functools

import jax
import jax.numpy as jnp
from jax import lax
from jax.experimental import pallas as pl
from jax.experimental.pallas import tpu as pltpu
from jax.sharding import Mesh, PartitionSpec as P

PAIRS_DEV = 256
HALF = PAIRS_DEV // 2
FIRST = (0, 1)
SECOND = (3, 2)


def shift(value, axis, step):
    size = lax.axis_size(axis)
    return lax.ppermute(value, axis, [(i, (i + step) % size) for i in range(size)])


def products_kernel(x_ref, a_ref, own_ref, other_ref, o_ref, acc_ref, *, relative_first):
    depth = own_ref.shape[1]
    acc_ref[...] = jnp.dot(
        a_ref[0, :, :depth], own_ref[0], preferred_element_type=jnp.float32
    ) + jnp.dot(a_ref[0, :, depth:], other_ref[0], preferred_element_type=jnp.float32)
    for rel in range(4):
        column = pl.multiple_of(lax.rem(x_ref[0] + rel, 4) * 128, 128)
        for half in range(2):
            tile = acc_ref[half * HALF : (half + 1) * HALF, pl.ds(column, 128)]
            if relative_first:
                o_ref[rel, half, 0, 0, 0] = tile
            else:
                o_ref[half, 0, 0, rel, 0] = tile


def products(operand, own, other, x_index, relative_first):
    if relative_first:
        out_shape = (4, 2, 2, 2, 2, HALF, 128)
        out_block = (4, 2, 1, 1, 1, HALF, 128)
        out_map = lambda c, zl, d, x: (0, 0, d, zl, c, 0, 0)
    else:
        out_shape = (2, 2, 2, 4, 2, HALF, 128)
        out_block = (2, 1, 1, 4, 1, HALF, 128)
        out_map = lambda c, zl, d, x: (0, d, zl, 0, c, 0, 0)
    rows, contracted = operand.shape[1:]
    return pl.pallas_call(
        functools.partial(products_kernel, relative_first=relative_first),
        grid_spec=pltpu.PrefetchScalarGridSpec(
            num_scalar_prefetch=1,
            grid=(2, 2, 2),
            in_specs=[
                pl.BlockSpec((1, rows, contracted), lambda c, zl, d, x: (d, 0, 0)),
                pl.BlockSpec((1, contracted // 2, 512), lambda c, zl, d, x: (c, 0, zl)),
                pl.BlockSpec((1, contracted // 2, 512), lambda c, zl, d, x: (c, 0, zl)),
            ],
            out_specs=pl.BlockSpec(out_block, out_map),
            scratch_shapes=[pltpu.VMEM((rows, 512), jnp.float32)],
        ),
        out_shape=jax.ShapeDtypeStruct(out_shape, jnp.float32),
        compiler_params=pltpu.CompilerParams(vmem_limit_bytes=32 * 1024 * 1024),
        cost_estimate=pl.CostEstimate(
            flops=2 * 2 * rows * contracted * 2048, bytes_accessed=16 * 1024 * 1024, transcendentals=0
        ),
    )(x_index, operand, own, other)


def sum_over_x(tiles):
    from_left = shift(tiles[2, 0], "x", 1)
    from_right = shift(tiles[2, 1], "x", -1)
    left_late = shift(tiles[1, 1], "x", 1)
    right_late = shift(tiles[3, 0], "x", -1)
    left_early = shift(tiles[1, 0] + from_left, "x", 1)
    right_early = shift(tiles[3, 1] + from_right, "x", -1)
    first = tiles[0, 0] + left_early + right_late
    second = tiles[0, 1] + left_late + right_early
    return jnp.stack([first, second])


def sum_over_z(tiles):
    up = shift(tiles[4, 0], "z", 1)
    down = shift(tiles[4, 1], "z", -1)
    up = shift(tiles[3] + jnp.stack([up, jnp.zeros_like(up)]), "z", 1)
    down = shift(tiles[5] + jnp.stack([jnp.zeros_like(down), down]), "z", -1)
    up = shift(tiles[2] + up, "z", 1)
    down = shift(tiles[6] + down, "z", -1)
    up = shift(tiles[1] + up, "z", 1)
    down = shift(tiles[7] + down, "z", -1)
    return tiles[0] + up + down


def placements():
    moves = ([], [])
    for y in range(4):
        for z in range(8):
            upper, d, zl = z // 4, (z % 4) // 2, z % 2
            first_target = ((2 * y + zl) * 4) + (y + FIRST[d]) % 4
            second_target = ((2 * y + zl) * 4) + (y + SECOND[d]) % 4
            moves[upper].append((z * 4 + y, first_target))
            moves[1 - upper].append((z * 4 + y, second_target))
    return moves


def body(amplitudes, tile_pairs, row_pairs, owner, integrals):
    pair, x, z = lax.axis_index("pair"), lax.axis_index("x"), lax.axis_index("z")
    tile_count = owner.shape[0]
    slot_width = integrals.shape[1]
    part_width = amplitudes.shape[1]
    own = integrals.reshape(integrals.shape[0], slot_width * part_width, -1)
    other = shift(own, "pair", 1)

    lookup = tile_pairs[:, None] == jnp.arange(tile_count, dtype=jnp.int32)[None, :]
    slots = jnp.sum(jnp.where(lookup, owner[None, :], 0), axis=1)
    place = row_pairs * tile_count + (slots - pair * slot_width) % tile_count
    local = (
        jnp.zeros((PAIRS_DEV * tile_count, part_width), jnp.bfloat16).at[place].set(amplitudes)
    ).reshape(PAIRS_DEV, tile_count * part_width)
    after = shift(local, "slab", -1)
    before = shift(local, "slab", 1)
    across = jnp.concatenate(
        [shift(after[:HALF], "slab", -1), shift(before[HALF:], "slab", 1)]
    )

    x_index = x.astype(jnp.int32).reshape(1)
    first = products(jnp.stack([local, after]), own, other, x_index, False)
    second = products(jnp.stack([before, across]), own, other, x_index, True)

    first = lax.psum_scatter(
        first.reshape(8, 4 * 2 * HALF, 128), "z", scatter_dimension=0, tiled=True
    ).reshape(4, 2, HALF, 128)
    first = sum_over_x(first)

    second = sum_over_x(second)
    second = second[::-1].reshape(8, 2, HALF, 128)
    second = lax.dynamic_slice_in_dim(jnp.concatenate([second, second]), z, 8, 0)
    second = sum_over_z(second)

    first = first.astype(jnp.bfloat16)
    second = second.astype(jnp.bfloat16)
    low = z < 4
    moves = placements()
    top = lax.ppermute(jnp.where(low, first, second), ("z", "slab"), moves[0])
    bottom = lax.ppermute(jnp.where(low, second, first), ("z", "slab"), moves[1])
    return jnp.concatenate([top, bottom], axis=1).transpose(1, 0, 2)


def solution(mesh):
    fine = Mesh(mesh.devices.reshape(2, 8, 4, 4), ("pair", "z", "x", "slab"))
    return jax.shard_map(
        body,
        mesh=fine,
        in_specs=(
            P(("pair", "slab"), ("z", "x")),
            P(("pair", "slab")),
            P(("pair", "slab")),
            P(),
            P(None, "pair", ("z", "x"), "slab"),
        ),
        out_specs=P(("pair", "slab"), None, ("z", "x")),
        check_vma=False,
    )
```

```python
import functools

import jax
import jax.numpy as jnp
from jax import lax
from jax.experimental import pallas as pl
from jax.experimental.pallas import tpu as pltpu
from jax.sharding import Mesh, PartitionSpec as P

PAIRS_DEV = 256
HALF = PAIRS_DEV // 2
DOMAIN = 8
LANES = 128
PACKED = (DOMAIN + 1) * LANES
FIRST = (0, 1)
SECOND = (3, 2)
MIB = 1024 * 1024


def shift(value, axis, step):
    size = lax.axis_size(axis)
    return lax.ppermute(value, axis, [(i, (i + step) % size) for i in range(size)])


def pack_kernel(owner_ref, base_ref, tile_ref, pair_ref, a_ref, o_ref):
    rows = a_ref.shape[0]
    count = owner_ref.shape[0]
    tiles = tile_ref[...]
    slots = jnp.zeros((1, rows), jnp.int32)
    for t in range(count):
        slots = jnp.where(tiles == t, owner_ref[t], slots)
    slots = lax.rem(slots - base_ref[0] + count, count)
    pairs = pair_ref[...]
    in_pair = lax.broadcasted_iota(jnp.int32, (PAIRS_DEV, rows), 0) == pairs
    in_slot = lax.broadcasted_iota(jnp.int32, (count, rows), 0) == slots
    pair_hot = in_pair.astype(jnp.float32).astype(jnp.bfloat16)
    slot_hot = in_slot.astype(jnp.float32)
    slot_hot_narrow = slot_hot.astype(jnp.bfloat16)
    contract_rows = (((1,), (1,)), ((), ()))
    present = lax.dot_general(
        pair_hot, slot_hot_narrow, contract_rows, preferred_element_type=jnp.float32
    )
    present_t = lax.dot_general(
        slot_hot_narrow, pair_hot, contract_rows, preferred_element_type=jnp.float32
    )
    row_id = lax.broadcasted_iota(jnp.int32, (count, count), 0)
    col_id = lax.broadcasted_iota(jnp.int32, (count, count), 1)
    upper = (row_id < col_id).astype(jnp.float32).astype(jnp.bfloat16)
    lower = (row_id > col_id).astype(jnp.float32).astype(jnp.bfloat16)
    before = jnp.dot(present.astype(jnp.bfloat16), upper, preferred_element_type=jnp.float32)
    before_t = jnp.dot(lower, present_t.astype(jnp.bfloat16), preferred_element_type=jnp.float32)
    by_row = jnp.dot(
        before_t.astype(jnp.bfloat16), pair_hot, preferred_element_type=jnp.float32
    )
    rank = jnp.sum(by_row * slot_hot, axis=0, keepdims=True).astype(jnp.int32)
    slot_id = lax.broadcasted_iota(jnp.int32, (PAIRS_DEV, count), 1).astype(jnp.float32)
    lane = lax.broadcasted_iota(jnp.int32, (PAIRS_DEV, LANES), 1)
    table = jnp.zeros((PAIRS_DEV, LANES), jnp.float32)
    pair_id = lax.broadcasted_iota(jnp.int32, (PAIRS_DEV, rows), 0)
    for i in range(DOMAIN):
        chosen = (pair_id == jnp.where(rank == i, pairs, -1)).astype(jnp.float32)
        o_ref[:, i * LANES : (i + 1) * LANES] = jnp.dot(
            chosen.astype(jnp.bfloat16), a_ref[...], preferred_element_type=jnp.float32
        ).astype(jnp.bfloat16)
        mine = jnp.where(before == i, present * slot_id, 0.0)
        table = jnp.where(lane == i, jnp.sum(mine, axis=1, keepdims=True), table)
    o_ref[:, DOMAIN * LANES :] = table.astype(jnp.bfloat16)


def pack(amplitudes, tile_pairs, row_pairs, owner, base):
    rows = amplitudes.shape[0]
    smem = pl.BlockSpec(memory_space=pltpu.SMEM)
    vmem = pl.BlockSpec(memory_space=pltpu.VMEM)
    return pl.pallas_call(
        pack_kernel,
        in_specs=[smem, smem, vmem, vmem, vmem],
        out_specs=vmem,
        out_shape=jax.ShapeDtypeStruct((PAIRS_DEV, PACKED), jnp.bfloat16),
        compiler_params=pltpu.CompilerParams(vmem_limit_bytes=32 * MIB),
        cost_estimate=pl.CostEstimate(flops=2 * rows * rows * LANES, bytes_accessed=2 * MIB, transcendentals=0),
    )(owner, base, tile_pairs.reshape(1, rows), row_pairs.reshape(1, rows), amplitudes)


def expand(piece, dense_ref, row):
    rows = piece.shape[0]
    count = dense_ref.shape[1] // LANES
    tiles = [piece[:, i * LANES : (i + 1) * LANES] for i in range(DOMAIN)]
    table = piece[:, DOMAIN * LANES :].astype(jnp.float32)
    slots = [jnp.broadcast_to(table[:, i : i + 1], (rows, LANES)) for i in range(DOMAIN)]
    for j in range(count):
        total = jnp.zeros((rows, LANES), jnp.bfloat16)
        for i in range(max(0, j - (count - DOMAIN)), min(DOMAIN - 1, j) + 1):
            mask = (slots[i] == j).astype(jnp.float32).astype(jnp.bfloat16)
            total = total + mask * tiles[i]
        dense_ref[row : row + rows, j * LANES : (j + 1) * LANES] = total


def products_kernel(at_ref, *refs, pieces, blocks, by_z):
    piece_refs, (own_ref, other_ref, o_ref, dense_ref, acc_ref) = refs[:pieces], refs[pieces:]
    step, zl = pl.program_id(0), pl.program_id(1)

    @pl.when((step == 0) & (zl == 0))
    def _():
        row = 0
        for ref in piece_refs:
            for start in range(0, ref.shape[0], HALF):
                expand(ref[start : start + HALF, :], dense_ref, row)
                row += HALF

    depth = own_ref.shape[1]
    acc_ref[...] = jnp.dot(
        dense_ref[:, :depth], own_ref[0], preferred_element_type=jnp.float32
    ) + jnp.dot(dense_ref[:, depth:], other_ref[0], preferred_element_type=jnp.float32)
    x, z = at_ref[0], at_ref[1]
    for d in range(blocks):
        for half in range(2):
            at = (2 * d + half) * HALF
            for rel in range(4):
                if by_z:
                    column = pl.multiple_of(lax.rem(x + rel, 4) * LANES, LANES)
                    tile = acc_ref[at : at + HALF, pl.ds(column, LANES)]
                    away = lax.rem(4 * d + 2 * (1 - half) + zl - z + 8, 8)
                    o_ref[away // 2, 0, 0, rel] = tile
                else:
                    o_ref[rel, d, half, 0, 0] = acc_ref[at : at + HALF, rel * LANES : (rel + 1) * LANES]


def products(packed, own, other, at, by_z):
    rows = sum(piece.shape[0] for piece in packed)
    blocks = rows // PAIRS_DEV
    contracted = 2 * own.shape[1]
    if by_z:
        out_shape = (4, 2, 2, 4, HALF, LANES)
        out_block = (4, 1, 1, 4, HALF, LANES)
        out_map = lambda c, zl, at: (0, lax.rem(zl + at[1], 2), c, 0, 0, 0)
    else:
        out_shape = (4, blocks, 2, 2, 2, HALF, LANES)
        out_block = (4, blocks, 2, 1, 1, HALF, LANES)
        out_map = lambda c, zl, at: (0, 0, 0, zl, c, 0, 0)
    return pl.pallas_call(
        functools.partial(products_kernel, pieces=len(packed), blocks=blocks, by_z=by_z),
        grid_spec=pltpu.PrefetchScalarGridSpec(
            num_scalar_prefetch=1,
            grid=(2, 2),
            in_specs=[pl.BlockSpec(piece.shape, lambda c, zl, at: (0, 0)) for piece in packed]
            + [pl.BlockSpec((1, contracted // 2, 512), lambda c, zl, at: (c, 0, zl))] * 2,
            out_specs=pl.BlockSpec(out_block, out_map),
            scratch_shapes=[
                pltpu.VMEM((rows, contracted), jnp.bfloat16),
                pltpu.VMEM((rows, 512), jnp.float32),
            ],
        ),
        out_shape=jax.ShapeDtypeStruct(out_shape, jnp.float32),
        compiler_params=pltpu.CompilerParams(vmem_limit_bytes=(24 if by_z else 56) * MIB),
        cost_estimate=pl.CostEstimate(
            flops=2 * rows * contracted * 2048,
            bytes_accessed=8 * MIB + rows * 8192,
            transcendentals=0,
        ),
    )(at, *packed, own, other)


def sum_over_x(tiles):
    from_left = shift(tiles[2, 0], "x", 1)
    from_right = shift(tiles[2, 1], "x", -1)
    left = shift(tiles[1] + jnp.stack([from_left, jnp.zeros_like(from_left)]), "x", 1)
    right = shift(tiles[3] + jnp.stack([jnp.zeros_like(from_right), from_right]), "x", -1)
    return tiles[0] + left + right


def sum_over_z(tiles):
    up = shift(tiles(4)[:2], "z", 1)
    down = shift(tiles(4)[2:], "z", -1)
    up = shift(tiles(3) + jnp.concatenate([up, jnp.zeros_like(up)]), "z", 1)
    down = shift(tiles(5) + jnp.concatenate([jnp.zeros_like(down), down]), "z", -1)
    up = shift(tiles(2) + up, "z", 1)
    down = shift(tiles(6) + down, "z", -1)
    up = shift(tiles(1) + up, "z", 1)
    down = shift(tiles(7) + down, "z", -1)
    return tiles(0) + up + down


def placements():
    moves = ([], [])
    for y in range(4):
        for z in range(8):
            d, bit, zl = z // 4, (z % 4) // 2, z % 2
            first_target = ((2 * y + zl) * 4) + (y + FIRST[d]) % 4
            second_target = ((2 * y + zl) * 4) + (y + SECOND[d]) % 4
            moves[bit].append((z * 4 + y, first_target))
            moves[1 - bit].append((z * 4 + y, second_target))
    return moves


def body(amplitudes, tile_pairs, row_pairs, owner, integrals):
    pair, x, z = lax.axis_index("pair"), lax.axis_index("x"), lax.axis_index("z")
    slot_width = integrals.shape[1]
    own = integrals.reshape(integrals.shape[0], slot_width * amplitudes.shape[1], -1)
    other = shift(own, "pair", 1)

    base = (pair * slot_width).astype(jnp.int32).reshape(1)
    local = pack(amplitudes, tile_pairs, row_pairs, owner, base)
    after = shift(local, "slab", -1)
    before = shift(local, "slab", 1)
    after, before = lax.optimization_barrier((after, before))
    across = [shift(after[:HALF], "slab", -1), shift(before[HALF:], "slab", 1)]

    at = jnp.stack([x, z]).astype(jnp.int32)
    firsts = [
        lax.psum_scatter(
            products([piece], own, other, at, False).reshape(4, -1, LANES),
            "x",
            scatter_dimension=0,
            tiled=True,
        ).reshape(4, 2 * HALF, LANES)
        for piece in (local, after)
    ]
    second = products([before, *across], own, other, at, True)

    chains = [
        sum_over_z(lambda away, c=c: second[away // 2, away % 2, c]) for c in range(2)
    ]
    second = sum_over_x(jnp.stack(chains, axis=1))
    first = lax.psum_scatter(
        jnp.concatenate(firsts), "z", scatter_dimension=0, tiled=True
    ).reshape(2, HALF, LANES)

    first = first.astype(jnp.bfloat16)
    second = second.astype(jnp.bfloat16)
    even = (z // 2) % 2 == 0
    moves = placements()
    top = lax.ppermute(jnp.where(even, first, second), ("z", "slab"), moves[0])
    bottom = lax.ppermute(jnp.where(even, second, first), ("z", "slab"), moves[1])
    return jnp.concatenate([top, bottom], axis=1).transpose(1, 0, 2)


def solution(mesh):
    fine = Mesh(mesh.devices.reshape(2, 8, 4, 4), ("pair", "z", "x", "slab"))
    return jax.shard_map(
        body,
        mesh=fine,
        in_specs=(
            P(("pair", "slab"), ("z", "x")),
            P(("pair", "slab")),
            P(("pair", "slab")),
            P(),
            P(None, "pair", ("z", "x"), "slab"),
        ),
        out_specs=P(("pair", "slab"), None, ("z", "x")),
        check_vma=False,
    )
```

```python
import functools

import jax
import jax.numpy as jnp
from jax import lax
from jax.experimental import pallas as pl
from jax.experimental.pallas import tpu as pltpu
from jax.sharding import Mesh, PartitionSpec as P

PAIRS_DEV = 256
HALF = PAIRS_DEV // 2
DOMAIN = 8
LANES = 128
PACKED = (DOMAIN + 1) * LANES
FIRST = (0, 1)
SECOND = (3, 2)
MIB = 1024 * 1024


def shift(value, axis, step):
    size = lax.axis_size(axis)
    return lax.ppermute(value, axis, [(i, (i + step) % size) for i in range(size)])


def pack_kernel(base_ref, owner_in, tile_in, pair_in, a_in, o_ref, owner_ref, tile_ref, pair_ref, a_ref, sem):
    arriving = [
        pltpu.make_async_copy(source, target, sem.at[i])
        for i, (source, target) in enumerate(
            ((owner_in, owner_ref), (tile_in, tile_ref), (pair_in, pair_ref), (a_in, a_ref))
        )
    ]
    for copy in arriving:
        copy.start()
    for copy in arriving[:3]:
        copy.wait()
    rows = a_ref.shape[0]
    count = owner_ref.shape[0]
    tiles = tile_ref[...]
    slots = jnp.zeros((1, rows), jnp.int32)
    for t in range(count):
        slots = jnp.where(tiles == t, owner_ref[t], slots)
    slots = lax.rem(slots - base_ref[0] + count, count)
    pairs = pair_ref[...]
    in_pair = lax.broadcasted_iota(jnp.int32, (PAIRS_DEV, rows), 0) == pairs
    in_slot = lax.broadcasted_iota(jnp.int32, (count, rows), 0) == slots
    pair_hot = in_pair.astype(jnp.float32).astype(jnp.bfloat16)
    slot_hot = in_slot.astype(jnp.float32)
    slot_hot_narrow = slot_hot.astype(jnp.bfloat16)
    contract_rows = (((1,), (1,)), ((), ()))
    present = lax.dot_general(
        pair_hot, slot_hot_narrow, contract_rows, preferred_element_type=jnp.float32
    )
    present_t = lax.dot_general(
        slot_hot_narrow, pair_hot, contract_rows, preferred_element_type=jnp.float32
    )
    row_id = lax.broadcasted_iota(jnp.int32, (count, count), 0)
    col_id = lax.broadcasted_iota(jnp.int32, (count, count), 1)
    upper = (row_id < col_id).astype(jnp.float32).astype(jnp.bfloat16)
    lower = (row_id > col_id).astype(jnp.float32).astype(jnp.bfloat16)
    before = jnp.dot(present.astype(jnp.bfloat16), upper, preferred_element_type=jnp.float32)
    before_t = jnp.dot(lower, present_t.astype(jnp.bfloat16), preferred_element_type=jnp.float32)
    by_row = jnp.dot(
        before_t.astype(jnp.bfloat16), pair_hot, preferred_element_type=jnp.float32
    )
    rank = jnp.sum(by_row * slot_hot, axis=0, keepdims=True).astype(jnp.int32)
    slot_id = lax.broadcasted_iota(jnp.int32, (PAIRS_DEV, count), 1).astype(jnp.float32)
    lane = lax.broadcasted_iota(jnp.int32, (PAIRS_DEV, LANES), 1)
    table = jnp.zeros((PAIRS_DEV, LANES), jnp.float32)
    pair_id = lax.broadcasted_iota(jnp.int32, (PAIRS_DEV, rows), 0)
    arriving[3].wait()
    for i in range(DOMAIN):
        chosen = (pair_id == jnp.where(rank == i, pairs, -1)).astype(jnp.float32)
        o_ref[:, i * LANES : (i + 1) * LANES] = jnp.dot(
            chosen.astype(jnp.bfloat16), a_ref[...], preferred_element_type=jnp.float32
        ).astype(jnp.bfloat16)
        mine = jnp.where(before == i, present * slot_id, 0.0)
        table = jnp.where(lane == i, jnp.sum(mine, axis=1, keepdims=True), table)
    o_ref[:, DOMAIN * LANES :] = table.astype(jnp.bfloat16)


SMEM = pl.BlockSpec(memory_space=pltpu.SMEM)
VMEM = pl.BlockSpec(memory_space=pltpu.VMEM)
HBM = pl.BlockSpec(memory_space=pltpu.HBM)
ANY = pl.BlockSpec(memory_space=pl.ANY)
SMALL = pl.CostEstimate(flops=1024, bytes_accessed=1024, transcendentals=0)


def pinned(space, *arrays):
    return [pltpu.with_memory_space_constraint(array, space) for array in arrays]


def pack(amplitudes, tile_pairs, row_pairs, owner, base):
    rows = amplitudes.shape[0]
    return pl.pallas_call(
        pack_kernel,
        in_specs=[SMEM, HBM, HBM, HBM, HBM],
        out_specs=VMEM,
        out_shape=jax.ShapeDtypeStruct((PAIRS_DEV, PACKED), jnp.bfloat16),
        scratch_shapes=[
            pltpu.SMEM(owner.shape, jnp.int32),
            pltpu.VMEM((1, rows), jnp.int32),
            pltpu.VMEM((1, rows), jnp.int32),
            pltpu.VMEM(amplitudes.shape, jnp.bfloat16),
            pltpu.SemaphoreType.DMA((4,)),
        ],
        compiler_params=pltpu.CompilerParams(vmem_limit_bytes=32 * MIB),
        cost_estimate=SMALL,
    )(
        base,
        *pinned(
            pltpu.HBM, owner, tile_pairs.reshape(1, rows), row_pairs.reshape(1, rows), amplitudes
        ),
    )


def expand(piece, dense_ref, row):
    rows = piece.shape[0]
    count = dense_ref.shape[1] // LANES
    tiles = [piece[:, i * LANES : (i + 1) * LANES] for i in range(DOMAIN)]
    table = piece[:, DOMAIN * LANES :].astype(jnp.float32)
    slots = [jnp.broadcast_to(table[:, i : i + 1], (rows, LANES)) for i in range(DOMAIN)]
    for j in range(count):
        total = jnp.zeros((rows, LANES), jnp.bfloat16)
        for i in range(max(0, j - (count - DOMAIN)), min(DOMAIN - 1, j) + 1):
            mask = (slots[i] == j).astype(jnp.float32).astype(jnp.bfloat16)
            total = total + mask * tiles[i]
        dense_ref[row : row + rows, j * LANES : (j + 1) * LANES] = total


def multiply(piece_refs, blocks, dense_ref, acc_ref, done):
    own_in, other_in, own_ref, other_ref, sem = blocks
    arriving = {}
    for c in range(2):
        for zl in range(2):
            columns = pl.ds(zl * 512, 512)
            arriving[c, zl] = [
                pltpu.make_async_copy(
                    source.at[c, :, columns], target.at[c, :, columns], sem.at[i, c, zl]
                )
                for i, (source, target) in enumerate(((own_in, own_ref), (other_in, other_ref)))
            ]
            for copy in arriving[c, zl]:
                copy.start()
    row = 0
    for ref in piece_refs:
        for start in range(0, ref.shape[0], HALF):
            expand(ref[start : start + HALF, :], dense_ref, row)
            row += HALF
    depth = own_ref.shape[1]
    for c in range(2):
        for zl in range(2):
            columns = slice(zl * 512, (zl + 1) * 512)
            slot = 2 * c + zl
            for copy in arriving[c, zl]:
                copy.wait()
            acc_ref[slot] = jnp.dot(
                dense_ref[:, :depth], own_ref[c, :, columns], preferred_element_type=jnp.float32
            ) + jnp.dot(
                dense_ref[:, depth:], other_ref[c, :, columns], preferred_element_type=jnp.float32
            )
            done(c, zl, slot)


def first_kernel(*refs, block, taken):
    at_ref, piece_ref, own_in, other_in = refs[:4]
    o_ref, own_ref, other_ref, block_sem, dense_ref, acc_ref, sem = refs[4 + taken :]
    blocks = (own_in, other_in, own_ref, other_ref, block_sem)
    x = at_ref[0]
    copies = []

    def done(c, zl, slot):
        for half in range(2):
            for column in range(4):
                copies.append(
                    pltpu.make_async_copy(
                        acc_ref.at[slot, pl.ds(half * HALF, HALF), pl.ds(column * LANES, LANES)],
                        o_ref.at[4 * block + 2 * half + zl, lax.rem(column - x + 4, 4), c],
                        sem.at[slot, half, column],
                    )
                )
                copies[-1].start()

    multiply([piece_ref], blocks, dense_ref, acc_ref, done)
    for copy in copies:
        copy.wait()


def second_kernel(*refs, pieces):
    at_ref, piece_refs, refs = refs[0], refs[1 : 1 + pieces], refs[1 + pieces :]
    own_in, other_in, t0_ref, t1_ref, t2a_ref, t2b_ref, t3_ref, *refs = refs
    own_ref, other_ref, block_sem, dense_ref, acc_ref = refs
    blocks = (own_in, other_in, own_ref, other_ref, block_sem)
    x = at_ref[0]

    def done(c, zl, slot):
        for rel in range(4):
            column = pl.multiple_of(lax.rem(x + rel, 4) * LANES, LANES)
            for half in range(2):
                tile = acc_ref[slot, half * HALF : (half + 1) * HALF, pl.ds(column, LANES)]
                if rel == 2:
                    (t2a_ref, t2b_ref)[half][zl, c] = tile
                else:
                    (t0_ref, t1_ref, None, t3_ref)[rel][half, zl, c] = tile

    multiply(piece_refs, blocks, dense_ref, acc_ref, done)


def product_scratch(own):
    return [
        pltpu.VMEM(own.shape, own.dtype),
        pltpu.VMEM(own.shape, own.dtype),
        pltpu.SemaphoreType.DMA((2, 2, 2)),
        pltpu.VMEM((PAIRS_DEV, 2 * own.shape[1]), jnp.bfloat16),
        pltpu.VMEM((4, PAIRS_DEV, 512), jnp.float32),
    ]


def first_products(piece, own, other, at, block, earlier):
    taken = [] if earlier is None else [earlier]
    return pl.pallas_call(
        functools.partial(first_kernel, block=block, taken=len(taken)),
        in_specs=[SMEM, VMEM, HBM, HBM] + [HBM] * len(taken),
        out_specs=HBM,
        out_shape=pltpu.HBM((8, 4, 2, HALF, LANES), jnp.float32),
        scratch_shapes=product_scratch(own) + [pltpu.SemaphoreType.DMA((4, 2, 4))],
        input_output_aliases={4: 0} if taken else {},
        compiler_params=pltpu.CompilerParams(vmem_limit_bytes=24 * MIB),
        cost_estimate=SMALL
        if taken
        else pl.CostEstimate(flops=2**32, bytes_accessed=16 * MIB, transcendentals=0),
    )(at, piece, *pinned(pltpu.HBM, own, other, *taken))


def second_products(packed, own, other, at):
    whole = jax.ShapeDtypeStruct((2, 2, 2, HALF, LANES), jnp.float32)
    part = jax.ShapeDtypeStruct((2, 2, HALF, LANES), jnp.float32)
    return pl.pallas_call(
        functools.partial(second_kernel, pieces=len(packed)),
        in_specs=[SMEM] + [VMEM] * len(packed) + [HBM] * 2,
        out_specs=[VMEM] * 5,
        out_shape=[whole, whole, part, part, whole],
        scratch_shapes=product_scratch(own),
        compiler_params=pltpu.CompilerParams(vmem_limit_bytes=24 * MIB),
        cost_estimate=SMALL,
    )(at, *packed, *pinned(pltpu.HBM, own, other))


def step_kernel(near_ref, far_ref, up_ref, down_ref, up_out, down_out):
    up_out[...] = near_ref[...]
    down_out[...] = far_ref[...]
    up_out[0] += up_ref[...]
    down_out[1] += down_ref[...]


def x_step(near, far, up, down):
    return pl.pallas_call(
        step_kernel,
        in_specs=[VMEM] * 4,
        out_specs=[VMEM] * 2,
        out_shape=[jax.ShapeDtypeStruct(near.shape, jnp.float32)] * 2,
        compiler_params=pltpu.CompilerParams(vmem_limit_bytes=16 * MIB),
        cost_estimate=SMALL,
    )(near, far, up, down)


def turn_kernel(at_ref, *refs):
    z = at_ref[1]
    out_ref, up_ref, down_ref = refs[6:]
    for d in range(2):
        own_ref, left_ref, right_ref = refs[3 * d : 3 * d + 3]
        for half in range(2):
            for zl in range(2):
                away = lax.rem(4 * d + 2 * (1 - half) + zl - z + 8, 8)
                out_ref[away] = own_ref[half, zl] + left_ref[half, zl] + right_ref[half, zl]
    up_ref[...] = out_ref[4, 0]
    down_ref[...] = out_ref[4, 1]


def turn(at, parts):
    tile = jax.ShapeDtypeStruct((HALF, LANES), jnp.float32)
    return pl.pallas_call(
        turn_kernel,
        in_specs=[SMEM] + [VMEM] * 6,
        out_specs=[VMEM] * 3,
        out_shape=[jax.ShapeDtypeStruct((8, 2, HALF, LANES), jnp.float32), tile, tile],
        compiler_params=pltpu.CompilerParams(vmem_limit_bytes=16 * MIB),
        cost_estimate=SMALL,
    )(at, *parts)


def z_step_kernel(tiles_ref, up_ref, down_ref, up_out, down_out, *, near):
    far = 8 - near
    if near == 3:
        up_out[0] = tiles_ref[near, 0] + up_ref[...]
        up_out[1] = tiles_ref[near, 1]
        down_out[0] = tiles_ref[far, 0]
        down_out[1] = tiles_ref[far, 1] + down_ref[...]
    else:
        up_out[...] = tiles_ref[near] + up_ref[...]
        down_out[...] = tiles_ref[far] + down_ref[...]


def z_step(tiles, up, down, near):
    return pl.pallas_call(
        functools.partial(z_step_kernel, near=near),
        in_specs=[VMEM] * 3,
        out_specs=[VMEM] * 2,
        out_shape=[jax.ShapeDtypeStruct((2, HALF, LANES), jnp.float32)] * 2,
        compiler_params=pltpu.CompilerParams(vmem_limit_bytes=16 * MIB),
        cost_estimate=SMALL,
    )(tiles, up, down)


def split_kernel(tiles_ref, after_ref, *refs):
    out_refs, sem = refs[:-1], refs[-1]
    copies = [
        pltpu.make_async_copy(tiles_ref.at[i], out_refs[i], sem.at[i]) for i in range(len(out_refs))
    ]
    for copy in copies:
        copy.start()
    for copy in copies:
        copy.wait()


def split(tiles, after):
    return pl.pallas_call(
        split_kernel,
        in_specs=[HBM, ANY],
        out_specs=[VMEM] * 4,
        out_shape=[jax.ShapeDtypeStruct(tiles.shape[1:], jnp.float32)] * 4,
        scratch_shapes=[pltpu.SemaphoreType.DMA((4,))],
        compiler_params=pltpu.CompilerParams(vmem_limit_bytes=16 * MIB),
        cost_estimate=SMALL,
    )(*pinned(pltpu.HBM, tiles), after)


def placements():
    moves = ([], [])
    for y in range(4):
        for z in range(8):
            d, bit, zl = z // 4, (z % 4) // 2, z % 2
            first_target = ((2 * y + zl) * 4) + (y + FIRST[d]) % 4
            second_target = ((2 * y + zl) * 4) + (y + SECOND[d]) % 4
            moves[bit].append((z * 4 + y, first_target))
            moves[1 - bit].append((z * 4 + y, second_target))
    return moves


def body(amplitudes, tile_pairs, row_pairs, owner, integrals):
    pair, x, z = lax.axis_index("pair"), lax.axis_index("x"), lax.axis_index("z")
    slot_width = integrals.shape[1]
    own = integrals.reshape(integrals.shape[0], slot_width * amplitudes.shape[1], -1)
    other = shift(own, "pair", 1)

    base = (pair * slot_width).astype(jnp.int32).reshape(1)
    local = pack(amplitudes, tile_pairs, row_pairs, owner, base)
    after = shift(local, "slab", -1)
    before = shift(local, "slab", 1)
    after, before = lax.optimization_barrier((after, before))
    across = [shift(after[:HALF], "slab", -1), shift(before[HALF:], "slab", 1)]

    at = jnp.stack([x, z]).astype(jnp.int32)
    first = first_products(local, own, other, at, 0, None)
    first = first_products(after, own, other, at, 1, first)
    first = lax.psum_scatter(
        first.reshape(8, -1, LANES), "z", scatter_dimension=0, tiled=True
    ).reshape(4, 2, HALF, LANES)

    parts = []
    for packed in ([before], across):
        t0, t1, t2a, t2b, t3 = second_products(packed, own, other, at)
        up, down = x_step(t1, t3, shift(t2a, "x", 1), shift(t2b, "x", -1))
        parts += [t0, shift(up, "x", 1), shift(down, "x", -1)]
    tiles, up, down = turn(at, parts)
    token = None
    for near in (3, 2, 1):
        up, down = z_step(tiles, shift(up, "z", 1), shift(down, "z", -1), near)
        token = up if near == 2 else token
    second = tiles[0] + shift(up, "z", 1) + shift(down, "z", -1)

    r0, r1, r2, r3 = split(first, token)
    first = r0 + shift(r1, "x", 1) + shift(r3, "x", -1) + shift(r2, "x", 2)

    first = first.astype(jnp.bfloat16)
    second = second.astype(jnp.bfloat16)
    even = (z // 2) % 2 == 0
    moves = placements()
    top = lax.ppermute(jnp.where(even, first, second), ("z", "slab"), moves[0])
    bottom = lax.ppermute(jnp.where(even, second, first), ("z", "slab"), moves[1])
    return jnp.concatenate([top, bottom], axis=1).transpose(1, 0, 2)


def solution(mesh):
    fine = Mesh(mesh.devices.reshape(2, 8, 4, 4), ("pair", "z", "x", "slab"))
    return jax.shard_map(
        body,
        mesh=fine,
        in_specs=(
            P(("pair", "slab"), ("z", "x")),
            P(("pair", "slab")),
            P(("pair", "slab")),
            P(),
            P(None, "pair", ("z", "x"), "slab"),
        ),
        out_specs=P(("pair", "slab"), None, ("z", "x")),
        check_vma=False,
    )
```
